32 devices in a mesh: rec: 16 (over z, y, x), var: 2 (over core).
Axes of the slice: x: 2, y: 2, z: 4, core: 2. Of those that a mesh axis runs over, the one named last changes fastest.
Arguments:
- records: bfloat16 [32768, 8192], P('rec', 'var'), as said below
- test_matrix: bfloat16 [8192, 256], P('var'), may hold values from -0.0625 to 0.0625
- col_types: int32 [8192], P('var'), may hold values from 0 to 1
- col_groups: int32 [8192], P('var'), may hold values from 0 to 15
- group_weight: float32 [16], replicated, may hold values from 0.5 to 2
Outputs:
- scores_basis: bfloat16 [32768, 256], P(('rec', 'var'))
- projection: bfloat16 [256, 8192], P(None, 'var')
The draws below stay inside these ranges and needn't reach their ends.
Inputs may be any that keep to these rules, and one draw needn't show every extreme that they name: `records`: every entry is positive.
All inputs are finite; a program needn't handle non-finite values.
Results may differ from the reference program's by a relative error of at most 0.0043.
The reference program's roundings to bfloat16 on the way count: a program that leaves them out, or rounds other values in their place, can miss the bound.
Values sent between devices are 32-bit elements; how exact they have to be, the bound alone decides.
A program may use at most 64 MiB of HBM per device.

```python
import math
import jax
import jax.numpy as jnp
from jax import lax

C = 8192
K = 256
GROUPS = 16
REC_DEV = 2048
NREC = 32768
N_REC = 16


def draw_records(key, part):
    key_centre, key_noise, key_spots, key_heavy = jax.random.split(key, 4)
    centre = jnp.exp(jax.random.uniform(key_centre, (C,), jnp.float32, math.log(0.3), math.log(3.0)))
    noise = jnp.clip(jax.random.normal(key_noise, (NREC, C), jnp.float32), -2.2, 2.2)
    rows = jnp.arange(NREC, dtype=jnp.int32)
    rising = 0.6 + 0.8 * rows.astype(jnp.float32) / NREC
    values = 1.0 + 0.3 * rising[:, None] * noise
    quarter = NREC // 4
    spots = jnp.arange(4, dtype=jnp.int32) * quarter + jax.random.randint(key_spots, (4,), 0, quarter)
    strength = 0.65 * math.sqrt(NREC / K)
    heavy = 1.0 + 0.3 * strength * 1.7 * jax.random.uniform(key_heavy, (4, C), jnp.float32, 0.0, 1.0)
    for spot_index in range(4):
        values = jnp.where((rows == spots[spot_index])[:, None], heavy[spot_index][None, :], values)
    return (centre[None, :] * values).astype(jnp.bfloat16)


def with_ends(result, stream_key, least, high):
    extent = result.shape
    index_at = [jax.random.randint(jax.random.fold_in(stream_key, axis), (), 0, extent[axis]) for axis in range(len(extent))]
    result = result.at[tuple(index_at)].set(least)
    longest = extent.index(max(extent))
    index_at[longest] = (index_at[longest] + 1) % extent[longest]
    return result.at[tuple(index_at)].set(high)


def steps_of(rng, extent, cuts, smallest, top_value):
    gain = 1.0
    for dim, parts in cuts:
        heights = jax.random.uniform(jax.random.fold_in(jax.random.fold_in(rng, 6), dim), (parts,), jnp.float32, smallest / len(cuts), top_value / len(cuts))
        gain = gain * jnp.repeat(jnp.exp(heights), extent[dim] // parts).reshape((-1,) + (1,) * (len(extent) - 1 - dim))
    return gain


def gaussian(key, shape, deviation, reach, shards=(), kind=jnp.bfloat16):
    drawn = jax.random.normal(key, shape, jnp.float32) * deviation
    if len(shards) > 0:
        drawn = steps_of(key, shape, shards, -0.22, 0.18) * drawn
    return jnp.clip(drawn, min=-reach, max=reach).astype(kind)


def setup_inputs(seed: int = 0) -> dict:
    key_of = jax.random.split(jax.random.key(seed), 6)
    records = draw_records(jax.random.fold_in(key_of[5], 71), 0)
    test_matrix = gaussian(key_of[1], (C, K), C ** -0.5, 0.0625, ((0, 2),))
    col_types = with_ends(jax.random.randint(key_of[2], (C,), 0, 2), jax.random.fold_in(key_of[2], 1), 0, 1).astype(jnp.int32)
    col_groups = with_ends(jax.random.randint(key_of[3], (C,), 0, GROUPS), jax.random.fold_in(key_of[3], 1), 0, GROUPS - 1).astype(jnp.int32)
    group_weight = jnp.clip(jnp.exp(jax.random.uniform(key_of[4], (GROUPS,), jnp.float32, math.log(0.5), math.log(2.0))), 0.5, 2.0)
    return {"records": records, "test_matrix": test_matrix, "col_types": col_types, "col_groups": col_groups, "group_weight": group_weight}


epsilon = 1e-05

def column_factor(col_mean, col_square, col_types, col_weight):
    spread = col_square - col_mean * col_mean
    picked = jnp.where(col_types == 1, lax.rsqrt(col_mean + epsilon), lax.rsqrt(spread + epsilon))
    return picked * col_weight

def reference(records, test_matrix, col_types, col_groups, group_weight):
    blocks = records.reshape(N_REC, REC_DEV, C)

    def stats(block):
        values = block.astype(jnp.float32)
        return (lax.optimization_barrier(jnp.sum(values, 0)), lax.optimization_barrier(jnp.sum(values * values, 0)))
    sums, squares = lax.map(stats, blocks)
    col_mean = lax.optimization_barrier(jnp.sum(sums, 0)) / NREC
    col_square = lax.optimization_barrier(jnp.sum(squares, 0)) / NREC
    col_weight = group_weight[col_groups]
    factor = column_factor(col_mean, col_square, col_types, col_weight)

    def scale_block(block):
        return ((block.astype(jnp.float32) - col_mean) * factor).astype(jnp.bfloat16)

    def sketch_block(block):
        return jnp.dot(scale_block(block).astype(jnp.float32), test_matrix.astype(jnp.float32), preferred_element_type=jnp.float32)
    sketch = lax.map(sketch_block, blocks).reshape(NREC, K)
    basis, upper = jnp.linalg.qr(sketch)
    basis = basis * jnp.sign(jnp.diagonal(upper))[None, :]

    def accumulate(running, pair):
        block, basis_block = pair
        term = jnp.dot(basis_block.T, scale_block(block).astype(jnp.float32), precision=lax.Precision.HIGHEST)
        return (running + term, None)
    projection, _ = lax.scan(accumulate, jnp.zeros((K, C), jnp.float32), (blocks, basis.reshape(N_REC, REC_DEV, K)))
    projection = projection / math.sqrt(NREC)
    return ((basis * math.sqrt(NREC)).astype(jnp.bfloat16), projection.astype(jnp.bfloat16))
```

```python
import functools
import math

import jax
import jax.numpy as jnp
from jax import lax
from jax.experimental import pallas as pl
from jax.experimental.pallas import tpu as pltpu
from jax.sharding import PartitionSpec as P

epsilon = 1e-05
highest = lax.Precision.HIGHEST
MESH = pl.DeviceIdType.MESH
LANES = 128
BLOCK = 64
QUARTERS = 4


def column_factor(col_mean, col_square, col_types, col_weight):
    spread = col_square - col_mean * col_mean
    picked = jnp.where(col_types == 1, lax.rsqrt(col_mean + epsilon), lax.rsqrt(spread + epsilon))
    return picked * col_weight


def rec_groups(n_rec):
    groups, shift = [], 1
    while shift < n_rec:
        size = min(4, n_rec // shift)
        groups.append((shift, size))
        shift *= size
    return groups


def group_place(me, shift, size):
    return lax.rem(lax.div(me, shift), size)


def greet(me, groups, my_var, n_var):
    barrier = pltpu.get_barrier_semaphore()
    count = 0
    for shift, size in groups:
        place = group_place(me, shift, size)
        for k in range(1, size):
            other = me + (lax.rem(place + k, size) - place) * shift
            pl.semaphore_signal(barrier, inc=1, device_id=(other, my_var), device_id_type=MESH)
            count += 1
    for k in range(1, n_var):
        pl.semaphore_signal(barrier, inc=1, device_id=(me, lax.rem(my_var + k, n_var)), device_id_type=MESH)
        count += 1
    pl.semaphore_wait(barrier, count)


def group_sum(value, buf, send_sem, recv_sem, me, my_var, shift, size):
    place = group_place(me, shift, size)
    buf[place] = value
    copies = []
    for k in range(1, size):
        other = me + (lax.rem(place + k, size) - place) * shift
        copy = pltpu.make_async_remote_copy(
            src_ref=buf.at[place], dst_ref=buf.at[place], send_sem=send_sem.at[k], recv_sem=recv_sem.at[k],
            device_id=(other, my_var), device_id_type=MESH)
        copy.start()
        copies.append(copy)
    for copy in copies:
        copy.wait()
    total = buf[0]
    for i in range(1, size):
        total = total + buf[i]
    return total


def stats_kernel(n_rec, x_ref, o_ref, buf, send_sem, recv_sem):
    me, my_var = lax.axis_index("rec"), lax.axis_index("var")
    groups = rec_groups(n_rec)
    greet(me, groups, my_var, 1)
    current = x_ref[...]
    for g, (shift, size) in enumerate(groups):
        current = group_sum(current, buf.at[g], send_sem.at[g], recv_sem.at[g], me, my_var, shift, size)
    o_ref[...] = current


def sum_over_rec(x, n_rec):
    n_groups = len(rec_groups(n_rec))
    return pl.pallas_call(
        functools.partial(stats_kernel, n_rec),
        out_shape=jax.ShapeDtypeStruct(x.shape, x.dtype),
        in_specs=[pl.BlockSpec(memory_space=pltpu.VMEM)],
        out_specs=pl.BlockSpec(memory_space=pltpu.VMEM),
        scratch_shapes=[
            pltpu.VMEM((n_groups, 4) + x.shape, jnp.float32),
            pltpu.SemaphoreType.DMA((n_groups, 4)),
            pltpu.SemaphoreType.DMA((n_groups, 4)),
        ],
        compiler_params=pltpu.CompilerParams(collective_id=0, has_side_effects=True, vmem_limit_bytes=16 << 20),
    )(x)


def rows_at(start, size):
    return pl.ds(pl.multiple_of(start, 8), size)


def lanes_at(start, size):
    return pl.ds(pl.multiple_of(start, LANES), size)


def factor_block(block):
    tiles_n = BLOCK // 8
    lane = lax.broadcasted_iota(jnp.int32, (8, LANES), 1)
    row = lax.broadcasted_iota(jnp.int32, (8, LANES), 0)
    tiles = []
    for t in range(tiles_n):
        eye = (lane == row + (BLOCK + 8 * t)).astype(jnp.float32)
        tiles.append(jnp.where(lane < BLOCK, block[8 * t:8 * t + 8, :], eye))
    for j in range(BLOCK - 1):
        own, sub = j // 8, j % 8
        pivot_row = tiles[own][sub:sub + 1, :]
        scaled_row = pivot_row / pivot_row[:, j:j + 1]
        if sub < 7:
            below = jnp.where(row > sub, jnp.broadcast_to(tiles[own][:, j:j + 1], (8, LANES)), 0.0)
            tiles[own] = tiles[own] - below * scaled_row
        for t in range(own + 1, tiles_n):
            tiles[t] = tiles[t] - tiles[t][:, j:j + 1] * scaled_row
    done = []
    for t in range(tiles_n):
        pivots = jnp.sum(jnp.where(lane == row + 8 * t, tiles[t], 0.0), axis=1, keepdims=True)
        done.append(tiles[t] / jnp.sqrt(pivots))
    whole = jnp.concatenate(done, axis=0)
    return pltpu.roll(whole, BLOCK, axis=1)[:, :BLOCK]


def stage_plan(n_rec, columns):
    bits = n_rec.bit_length() - 1
    high = list(range(bits - 1, 1, -1))
    orders = [[0, 1] + high, [1, 0] + high]
    halvings = min(bits, (columns // (2 * LANES)).bit_length() - 1)
    return orders, halvings


def main_kernel(n_rec, n_var, total_rows, s_ref, y_ref, scores_ref, out_ref,
                y_buf, got, full, gram, gram_rs, gram_ar, aug,
                rs_send, rs_recv, ag_send, ag_recv, g_send, g_recv, y_sem):
    me, my_var = lax.axis_index("rec"), lax.axis_index("var")
    k_dim, columns = y_buf.shape
    groups = rec_groups(n_rec)
    orders, halvings = stage_plan(n_rec, columns)
    n_stages = len(orders[0])
    part_cols = columns // 2
    part_rows = k_dim // QUARTERS
    load = pltpu.make_async_copy(y_ref, y_buf, y_sem)
    load.start()

    greet(me, groups, my_var, n_var)

    def bit_of(j):
        return lax.rem(lax.div(me, 1 << j), 2)

    def peer_of(j):
        return me + (1 - 2 * bit_of(j)) * (1 << j)

    bases = []
    for p in range(2):
        base, held, width = [jnp.int32(p * part_cols)], [part_cols], part_cols
        for s in range(halvings):
            width //= 2
            base.append(base[-1] + bit_of(orders[p][s]) * width)
            held.append(width)
        for s in range(halvings, n_stages):
            base.append(base[-1])
            held.append(width)
        bases.append((base, held))
    got_at, at = [], 0
    for s in range(n_stages):
        got_at.append(at)
        at += bases[0][1][s + 1]

    def rs_copy(p, q, s):
        base, held = bases[p]
        width = held[s + 1]
        if s < halvings:
            start = base[s] + (1 - bit_of(orders[p][s])) * width
        else:
            start = base[s]
        rows = pl.ds(q * part_rows, part_rows)
        return pltpu.make_async_remote_copy(
            src_ref=y_buf.at[rows, lanes_at(start, width)],
            dst_ref=got.at[p, rows, pl.ds(got_at[s], width)],
            send_sem=rs_send.at[p, q, s], recv_sem=rs_recv.at[p, q, s],
            device_id=(peer_of(orders[p][s]), my_var), device_id_type=MESH)

    def rs_step(t):
        for q in range(QUARTERS):
            s = t - q
            if s < 0 or s > n_stages:
                continue
            for p in range(2):
                if s > 0:
                    rs_copy(p, q, s - 1).wait()
                    base, held = bases[p]
                    rows = pl.ds(q * part_rows, part_rows)
                    lanes = lanes_at(base[s], held[s])
                    y_buf[rows, lanes] = y_buf[rows, lanes] + got[p, rows, pl.ds(got_at[s - 1], held[s])]
                if s < n_stages:
                    rs_copy(p, q, s).start()

    rs_left = list(range(QUARTERS + n_stages))

    def advance(n=1):
        for _ in range(n):
            if rs_left:
                rs_step(rs_left.pop(0))

    rows_dev = s_ref.shape[0]
    step_rows = 256

    def gram_step(i, total):
        part = s_ref[rows_at(i * step_rows, step_rows), :]
        return total + lax.dot_general(part, part, (((0,), (0,)), ((), ())), precision=highest,
                                       preferred_element_type=jnp.float32)

    gram[0] = lax.fori_loop(0, rows_dev // step_rows, gram_step, jnp.zeros((k_dim, k_dim), jnp.float32))
    half = k_dim // n_var
    shift, size = groups[0]
    piece = half // size
    place = group_place(me, shift, size)
    copies = []
    for k in range(1, size):
        other_place = lax.rem(place + k, size)
        copy = pltpu.make_async_remote_copy(
            src_ref=gram.at[0, rows_at(my_var * half + other_place * piece, piece), :],
            dst_ref=gram_rs.at[place],
            send_sem=g_send.at[0, k], recv_sem=g_recv.at[0, k],
            device_id=(me + (other_place - place) * shift, my_var), device_id_type=MESH)
        copy.start()
        copies.append(copy)
    own_rows = rows_at(my_var * half + place * piece, piece)
    gram_rs[place] = gram[0, own_rows, :]
    load.wait()
    for copy in copies:
        copy.wait()
    current = gram_rs[0]
    for i in range(1, size):
        current = current + gram_rs[i]
    for g in range(1, len(groups)):
        current = group_sum(current, gram_ar.at[g - 1], g_send.at[g], g_recv.at[g], me, my_var, *groups[g])
    gram[1, own_rows, :] = current
    copies = []
    last = len(groups)
    for k in range(1, size):
        other_place = lax.rem(place + k, size)
        copy = pltpu.make_async_remote_copy(
            src_ref=gram.at[1, own_rows, :], dst_ref=gram.at[1, own_rows, :],
            send_sem=g_send.at[last, k], recv_sem=g_recv.at[last, k],
            device_id=(me + (other_place - place) * shift, my_var), device_id_type=MESH)
        copy.start()
        copies.append(copy)
    for copy in copies:
        copy.wait()
    copies = []
    half_rows = rows_at(my_var * half, half)
    for k in range(1, n_var):
        copy = pltpu.make_async_remote_copy(
            src_ref=gram.at[1, half_rows, :], dst_ref=gram.at[1, half_rows, :],
            send_sem=g_send.at[last + 1, k], recv_sem=g_recv.at[last + 1, k],
            device_id=(me, lax.rem(my_var + k, n_var)), device_id_type=MESH)
        copy.start()
        copies.append(copy)
    advance()
    for copy in copies:
        copy.wait()

    aug[:, :k_dim] = gram[1]
    wide_row = lax.broadcasted_iota(jnp.int32, (k_dim, k_dim), 0)
    wide_lane = lax.broadcasted_iota(jnp.int32, (k_dim, k_dim), 1)
    aug[:, k_dim:] = (wide_row == wide_lane).astype(jnp.float32)
    n_blocks = k_dim // BLOCK
    for b in range(n_blocks):
        rows = slice(b * BLOCK, (b + 1) * BLOCK)
        lane_at = b * BLOCK // LANES * LANES
        block = aug[rows, lane_at:lane_at + LANES]
        if b * BLOCK != lane_at:
            block = pltpu.roll(block, LANES - BLOCK, axis=1)
        inverse = factor_block(block)
        advance()
        solved = jnp.dot(inverse, aug[rows, :], precision=highest, preferred_element_type=jnp.float32)
        aug[rows, :] = solved
        if b + 1 < n_blocks:
            change = lax.dot_general(solved[:, :k_dim], solved, (((0,), (0,)), ((), ())), precision=highest,
                                     preferred_element_type=jnp.float32)
            rest = slice((b + 1) * BLOCK, k_dim)
            aug[rest, :] = aug[rest, :] - change[rest, :]
            advance()
    advance(len(rs_left))

    for p in range(2):
        base, held = bases[p]
        lanes = lanes_at(base[-1], held[-1])
        full[:, lanes] = jnp.dot(aug[:, k_dim:], y_buf[:, lanes], precision=highest,
                                 preferred_element_type=jnp.float32) * (1.0 / math.sqrt(total_rows))

    def ag_copy(p, q, s):
        base, held = bases[p]
        place_now = (pl.ds(q * part_rows, part_rows), lanes_at(base[s + 1], held[s + 1]))
        return pltpu.make_async_remote_copy(
            src_ref=full.at[place_now], dst_ref=full.at[place_now],
            send_sem=ag_send.at[p, q, s], recv_sem=ag_recv.at[p, q, s],
            device_id=(peer_of(orders[p][s]), my_var), device_id_type=MESH)

    own = rows_dev // n_var
    for t in range(QUARTERS + halvings):
        for q in range(QUARTERS):
            s = halvings - 1 - (t - q)
            if s < -1 or s > halvings - 1:
                continue
            for p in range(2):
                if s < halvings - 1:
                    ag_copy(p, q, s + 1).wait()
                if s >= 0:
                    ag_copy(p, q, s).start()
            if s == -1:
                rows = slice(q * part_rows, (q + 1) * part_rows)
                out_ref[rows, :] = full[rows, :].astype(out_ref.dtype)
        if t < 4:
            n = own // 4
            mine = s_ref[rows_at(my_var * own + t * n, n), :]
            basis = lax.dot_general(mine, aug[:, k_dim:], (((1,), (1,)), ((), ())), precision=highest,
                                    preferred_element_type=jnp.float32)
            scores_ref[t * n:(t + 1) * n, :] = (basis * math.sqrt(total_rows)).astype(scores_ref.dtype)


def factor_and_project(sketch, products, n_rec, n_var, total_rows):
    rows_dev, k_dim = sketch.shape
    columns = products.shape[1]
    groups = rec_groups(n_rec)
    orders, halvings = stage_plan(n_rec, columns)
    n_stages = len(orders[0])
    width, got_width = columns // 2, 0
    for s in range(n_stages):
        if s < halvings:
            width //= 2
        got_width += width
    piece = k_dim // n_var // groups[0][1]
    vmem = pl.BlockSpec(memory_space=pltpu.VMEM)
    dma = pltpu.SemaphoreType.DMA
    return pl.pallas_call(
        functools.partial(main_kernel, n_rec, n_var, total_rows),
        out_shape=(
            jax.ShapeDtypeStruct((rows_dev // n_var, k_dim), jnp.bfloat16),
            jax.ShapeDtypeStruct((k_dim, columns), jnp.bfloat16),
        ),
        in_specs=[vmem, pl.BlockSpec(memory_space=pl.ANY)],
        out_specs=(vmem, vmem),
        scratch_shapes=[
            pltpu.VMEM((k_dim, columns), jnp.float32),
            pltpu.VMEM((2, k_dim, got_width), jnp.float32),
            pltpu.VMEM((k_dim, columns), jnp.float32),
            pltpu.VMEM((2, k_dim, k_dim), jnp.float32),
            pltpu.VMEM((groups[0][1], piece, k_dim), jnp.float32),
            pltpu.VMEM((max(1, len(groups) - 1), 4, piece, k_dim), jnp.float32),
            pltpu.VMEM((k_dim, 2 * k_dim), jnp.float32),
            dma((2, QUARTERS, n_stages)), dma((2, QUARTERS, n_stages)),
            dma((2, QUARTERS, n_stages)), dma((2, QUARTERS, n_stages)),
            dma((len(groups) + 2, max(4, n_var))), dma((len(groups) + 2, max(4, n_var))),
            dma,
        ],
        compiler_params=pltpu.CompilerParams(collective_id=1, has_side_effects=True, vmem_limit_bytes=48 << 20),
    )(sketch, products)


def local(records, test_matrix, col_types, col_groups, group_weight):
    n_rec, n_var = lax.axis_size("rec"), lax.axis_size("var")
    total_rows = records.shape[0] * n_rec
    columns = records.shape[1]
    values = records.astype(jnp.float32)
    sums = jnp.concatenate([jnp.sum(values, 0), jnp.sum(values * values, 0)]).reshape(-1, LANES)
    sums = sum_over_rec(sums, n_rec).reshape(2, columns)
    col_mean = sums[0] / total_rows
    onehot = (
        col_groups[:, None] == jnp.arange(group_weight.shape[0], dtype=jnp.int32)[None, :]
    ).astype(jnp.float32)
    col_weight = jnp.dot(onehot, group_weight, precision=highest)
    factor = column_factor(col_mean, sums[1] / total_rows, col_types, col_weight)
    scaled = ((values - col_mean) * factor).astype(jnp.bfloat16)
    partial_sketch = jnp.dot(scaled, test_matrix, preferred_element_type=jnp.float32)
    sketch = lax.psum(partial_sketch, "var")
    upper = sketch.astype(jnp.bfloat16)
    lower = (sketch - upper.astype(jnp.float32)).astype(jnp.bfloat16)
    both = jnp.concatenate([upper, lower], axis=1)
    pair = lax.dot_general(both, scaled, (((0,), (0,)), ((), ())), preferred_element_type=jnp.float32)
    k_dim = test_matrix.shape[1]
    products = pair[:k_dim] + pair[k_dim:]
    return factor_and_project(sketch, products, n_rec, n_var, total_rows)


def solution(mesh):
    in_specs = (P("rec", "var"), P("var", None), P("var"), P("var"), P())
    out_specs = (P(("rec", "var"), None), P(None, "var"))
    return jax.shard_map(local, mesh=mesh, in_specs=in_specs, out_specs=out_specs, check_vma=False)
```

```python
import functools
import math

import jax
import jax.numpy as jnp
from jax import lax
from jax.experimental import pallas as pl
from jax.experimental.pallas import tpu as pltpu
from jax.sharding import PartitionSpec as P

epsilon = 1e-05
highest = lax.Precision.HIGHEST
MESH = pl.DeviceIdType.MESH
LANES = 128
BLOCK = 64
QUARTERS = 4
TILE = 256
CHUNKS = 4


def column_factor(col_mean, col_square, col_types, col_weight):
    spread = col_square - col_mean * col_mean
    picked = jnp.where(col_types == 1, lax.rsqrt(col_mean + epsilon), lax.rsqrt(spread + epsilon))
    return picked * col_weight


def rec_groups(n_rec):
    groups, shift = [], 1
    while shift < n_rec:
        size = min(4, n_rec // shift)
        groups.append((shift, size))
        shift *= size
    return groups


def group_place(me, shift, size):
    return lax.rem(lax.div(me, shift), size)


def greet(me, groups, my_var, n_var):
    barrier = pltpu.get_barrier_semaphore()
    count = 0
    for shift, size in groups:
        place = group_place(me, shift, size)
        for k in range(1, size):
            other = me + (lax.rem(place + k, size) - place) * shift
            pl.semaphore_signal(barrier, inc=1, device_id=(other, my_var), device_id_type=MESH)
            count += 1
    for k in range(1, n_var):
        pl.semaphore_signal(barrier, inc=1, device_id=(me, lax.rem(my_var + k, n_var)), device_id_type=MESH)
        count += 1
    pl.semaphore_wait(barrier, count)


def group_start(value, buf, send_sem, recv_sem, me, my_var, shift, size):
    place = group_place(me, shift, size)
    buf[place] = value
    copies = []
    for k in range(1, size):
        other = me + (lax.rem(place + k, size) - place) * shift
        copy = pltpu.make_async_remote_copy(
            src_ref=buf.at[place], dst_ref=buf.at[place], send_sem=send_sem.at[k], recv_sem=recv_sem.at[k],
            device_id=(other, my_var), device_id_type=MESH)
        copy.start()
        copies.append(copy)
    return copies


def group_finish(buf, copies):
    for copy in copies:
        copy.wait()
    total = buf[0]
    for i in range(1, len(copies) + 1):
        total = total + buf[i]
    return total


def stats_kernel(n_rec, x_ref, o_ref, buf, send_sem, recv_sem):
    me, my_var = lax.axis_index("rec"), lax.axis_index("var")
    groups = rec_groups(n_rec)
    greet(me, groups, my_var, 1)
    current = x_ref[...]
    for g, (shift, size) in enumerate(groups):
        sent = group_start(current, buf.at[g], send_sem.at[g], recv_sem.at[g], me, my_var, shift, size)
        current = group_finish(buf.at[g], sent)
    o_ref[...] = current


def sum_over_rec(x, n_rec):
    n_groups = len(rec_groups(n_rec))
    return pl.pallas_call(
        functools.partial(stats_kernel, n_rec),
        out_shape=jax.ShapeDtypeStruct(x.shape, x.dtype),
        in_specs=[pl.BlockSpec(memory_space=pltpu.VMEM)],
        out_specs=pl.BlockSpec(memory_space=pltpu.VMEM),
        scratch_shapes=[
            pltpu.VMEM((n_groups, 4) + x.shape, jnp.float32),
            pltpu.SemaphoreType.DMA((n_groups, 4)),
            pltpu.SemaphoreType.DMA((n_groups, 4)),
        ],
        compiler_params=pltpu.CompilerParams(collective_id=0, has_side_effects=True, vmem_limit_bytes=16 << 20),
    )(x)


def rows_at(start, size):
    return pl.ds(pl.multiple_of(start, 8), size)


def lanes_at(start, size):
    return pl.ds(pl.multiple_of(start, LANES), size)


def factor_block(block):
    tiles_n = BLOCK // 8
    lane = lax.broadcasted_iota(jnp.int32, (8, LANES), 1)
    row = lax.broadcasted_iota(jnp.int32, (8, LANES), 0)
    tiles = []
    for t in range(tiles_n):
        eye = (lane == row + (BLOCK + 8 * t)).astype(jnp.float32)
        tiles.append(jnp.where(lane < BLOCK, block[8 * t:8 * t + 8, :], eye))
    for j in range(BLOCK - 1):
        own, sub = j // 8, j % 8
        pivot_row = tiles[own][sub:sub + 1, :]
        scaled_row = pivot_row / pivot_row[:, j:j + 1]
        if sub < 7:
            below = jnp.where(row > sub, jnp.broadcast_to(tiles[own][:, j:j + 1], (8, LANES)), 0.0)
            tiles[own] = tiles[own] - below * scaled_row
        for t in range(own + 1, tiles_n):
            tiles[t] = tiles[t] - tiles[t][:, j:j + 1] * scaled_row
    done = []
    for t in range(tiles_n):
        pivots = jnp.sum(jnp.where(lane == row + 8 * t, tiles[t], 0.0), axis=1, keepdims=True)
        done.append(tiles[t] / jnp.sqrt(pivots))
    whole = jnp.concatenate(done, axis=0)
    return pltpu.roll(whole, BLOCK, axis=1)[:, :BLOCK]


def stage_plan(n_rec, columns):
    bits = n_rec.bit_length() - 1
    high = list(range(bits - 1, 1, -1))
    orders = [[0, 1] + high, [1, 0] + high]
    halvings = min(bits, (columns // (2 * LANES)).bit_length() - 1)
    return orders, halvings


def main_kernel(n_rec, n_var, total_rows, part_ref, mean_ref, factor_ref, rec_ref, scores_ref, out_ref,
                s_ref, s_got, s_pair, raw, tile, y_buf, got, full, gram, gram_rs, gram_ar, aug,
                rs_send, rs_recv, ag_send, ag_recv, g_send, g_recv, s_send, s_recv, raw_sem):
    me, my_var = lax.axis_index("rec"), lax.axis_index("var")
    k_dim, columns = y_buf.shape
    groups = rec_groups(n_rec)
    orders, halvings = stage_plan(n_rec, columns)
    n_stages = len(orders[0])
    part_cols = columns // 2
    part_rows = k_dim // QUARTERS
    n_tiles = columns // TILE
    rows_dev = s_ref.shape[0]
    chunk = rows_dev // CHUNKS

    def raw_copy(i, slot):
        return pltpu.make_async_copy(rec_ref.at[:, lanes_at(i * TILE, TILE)], raw.at[slot], raw_sem.at[slot])

    raw_copy(0, 0).start()
    greet(me, groups, my_var, n_var)

    def sketch_copy(c):
        rows = pl.ds(c * chunk, chunk)
        return pltpu.make_async_remote_copy(
            src_ref=part_ref.at[rows, :], dst_ref=s_got.at[rows, :], send_sem=s_send.at[c], recv_sem=s_recv.at[c],
            device_id=(me, 1 - my_var), device_id_type=MESH)

    if n_var == 2:
        for c in range(CHUNKS):
            sketch_copy(c).start()

    def bit_of(j):
        return lax.rem(lax.div(me, 1 << j), 2)

    def peer_of(j):
        return me + (1 - 2 * bit_of(j)) * (1 << j)

    bases = []
    for p in range(2):
        base, held, width = [jnp.int32(p * part_cols)], [part_cols], part_cols
        for s in range(halvings):
            width //= 2
            base.append(base[-1] + bit_of(orders[p][s]) * width)
            held.append(width)
        for s in range(halvings, n_stages):
            base.append(base[-1])
            held.append(width)
        bases.append((base, held))
    got_at, at = [], 0
    for s in range(n_stages):
        got_at.append(at)
        at += bases[0][1][s + 1]

    def rs_copy(p, q, s):
        base, held = bases[p]
        width = held[s + 1]
        if s < halvings:
            start = base[s] + (1 - bit_of(orders[p][s])) * width
        else:
            start = base[s]
        rows = pl.ds(q * part_rows, part_rows)
        return pltpu.make_async_remote_copy(
            src_ref=y_buf.at[rows, lanes_at(start, width)],
            dst_ref=got.at[p, rows, pl.ds(got_at[s], width)],
            send_sem=rs_send.at[p, q, s], recv_sem=rs_recv.at[p, q, s],
            device_id=(peer_of(orders[p][s]), my_var), device_id_type=MESH)

    def rs_step(t):
        for q in range(QUARTERS):
            s = t - q
            if s < 0 or s > n_stages:
                continue
            for p in range(2):
                if s > 0:
                    rs_copy(p, q, s - 1).wait()
                    base, held = bases[p]
                    rows = pl.ds(q * part_rows, part_rows)
                    lanes = lanes_at(base[s], held[s])
                    y_buf[rows, lanes] = y_buf[rows, lanes] + got[p, rows, pl.ds(got_at[s - 1], held[s])]
                if 0 < s < n_stages:
                    rs_copy(p, q, s).start()

    def rs_begin(p, q):
        rs_copy(p, q, 0).start()

    rs_left = list(range(QUARTERS + n_stages))

    def advance(n=1):
        for _ in range(n):
            if rs_left:
                rs_step(rs_left.pop(0))

    total = jnp.zeros((k_dim, k_dim), jnp.float32)
    for c in range(CHUNKS):
        rows = pl.ds(c * chunk, chunk)
        part = part_ref[rows, :]
        if n_var == 2:
            sketch_copy(c).wait()
            part = part + s_got[rows, :]
        s_ref[rows, :] = part
        turned = part.T
        upper = turned.astype(jnp.bfloat16)
        s_pair[:k_dim, rows] = upper
        s_pair[k_dim:, rows] = (turned - upper.astype(jnp.float32)).astype(jnp.bfloat16)
        total = total + jnp.dot(turned, part, precision=highest, preferred_element_type=jnp.float32)
    gram[0] = total

    def products(first, last):
        def one(i, carry):
            slot = lax.rem(i, 2)

            @pl.when(i + 1 < n_tiles)
            def _():
                raw_copy(i + 1, 1 - slot).start()

            raw_copy(i, slot).wait()
            lanes = lanes_at(i * TILE, TILE)
            mean, factor = mean_ref[:, lanes], factor_ref[:, lanes]
            for c in range(CHUNKS):
                rows = pl.ds(c * chunk, chunk)
                tile[rows, :] = ((raw[slot, rows, :].astype(jnp.float32) - mean) * factor).astype(jnp.bfloat16)
            pair = jnp.dot(s_pair[...], tile[...], preferred_element_type=jnp.float32)
            y_buf[:, lanes] = pair[:k_dim] + pair[k_dim:]
            return carry

        lax.fori_loop(first, last, one, 0)

    half = k_dim // n_var
    shift, size = groups[0]
    piece = half // size
    place = group_place(me, shift, size)
    cuts = [n_tiles * i // 4 for i in range(5)]
    copies = []
    for k in range(1, size):
        other_place = lax.rem(place + k, size)
        copy = pltpu.make_async_remote_copy(
            src_ref=gram.at[0, rows_at(my_var * half + other_place * piece, piece), :],
            dst_ref=gram_rs.at[place],
            send_sem=g_send.at[0, k], recv_sem=g_recv.at[0, k],
            device_id=(me + (other_place - place) * shift, my_var), device_id_type=MESH)
        copy.start()
        copies.append(copy)
    own_rows = rows_at(my_var * half + place * piece, piece)
    gram_rs[place] = gram[0, own_rows, :]
    products(cuts[0], cuts[1])
    for copy in copies:
        copy.wait()
    current = gram_rs[0]
    for i in range(1, size):
        current = current + gram_rs[i]
    for g in range(1, len(groups)):
        sent = group_start(current, gram_ar.at[g - 1], g_send.at[g], g_recv.at[g], me, my_var, *groups[g])
        if g == 1:
            products(cuts[1], cuts[2])
        current = group_finish(gram_ar.at[g - 1], sent)
    gram[1, own_rows, :] = current
    copies = []
    last = len(groups)
    for k in range(1, size):
        other_place = lax.rem(place + k, size)
        copy = pltpu.make_async_remote_copy(
            src_ref=gram.at[1, own_rows, :], dst_ref=gram.at[1, own_rows, :],
            send_sem=g_send.at[last, k], recv_sem=g_recv.at[last, k],
            device_id=(me + (other_place - place) * shift, my_var), device_id_type=MESH)
        copy.start()
        copies.append(copy)
    for q in range(QUARTERS):
        rs_begin(0, q)
    products(cuts[2], cuts[3])
    for copy in copies:
        copy.wait()
    copies = []
    half_rows = rows_at(my_var * half, half)
    for k in range(1, n_var):
        copy = pltpu.make_async_remote_copy(
            src_ref=gram.at[1, half_rows, :], dst_ref=gram.at[1, half_rows, :],
            send_sem=g_send.at[last + 1, k], recv_sem=g_recv.at[last + 1, k],
            device_id=(me, lax.rem(my_var + k, n_var)), device_id_type=MESH)
        copy.start()
        copies.append(copy)
    products(cuts[3], cuts[4])
    for q in range(QUARTERS):
        rs_begin(1, q)
    rs_left.pop(0)
    for copy in copies:
        copy.wait()

    aug[:, :k_dim] = gram[1]
    wide_row = lax.broadcasted_iota(jnp.int32, (k_dim, k_dim), 0)
    wide_lane = lax.broadcasted_iota(jnp.int32, (k_dim, k_dim), 1)
    aug[:, k_dim:] = (wide_row == wide_lane).astype(jnp.float32)
    n_blocks = k_dim // BLOCK
    for b in range(n_blocks):
        rows = slice(b * BLOCK, (b + 1) * BLOCK)
        lane_at = b * BLOCK // LANES * LANES
        block = aug[rows, lane_at:lane_at + LANES]
        if b * BLOCK != lane_at:
            block = pltpu.roll(block, LANES - BLOCK, axis=1)
        inverse = factor_block(block)
        advance()
        solved = jnp.dot(inverse, aug[rows, :], precision=highest, preferred_element_type=jnp.float32)
        aug[rows, :] = solved
        if b + 1 < n_blocks:
            change = lax.dot_general(solved[:, :k_dim], solved, (((0,), (0,)), ((), ())), precision=highest,
                                     preferred_element_type=jnp.float32)
            rest = slice((b + 1) * BLOCK, k_dim)
            aug[rest, :] = aug[rest, :] - change[rest, :]
            advance()
    advance(len(rs_left))

    for p in range(2):
        base, held = bases[p]
        lanes = lanes_at(base[-1], held[-1])
        full[:, lanes] = jnp.dot(aug[:, k_dim:], y_buf[:, lanes], precision=highest,
                                 preferred_element_type=jnp.float32) * (1.0 / math.sqrt(total_rows))

    def ag_copy(p, q, s):
        base, held = bases[p]
        place_now = (pl.ds(q * part_rows, part_rows), lanes_at(base[s + 1], held[s + 1]))
        return pltpu.make_async_remote_copy(
            src_ref=full.at[place_now], dst_ref=full.at[place_now],
            send_sem=ag_send.at[p, q, s], recv_sem=ag_recv.at[p, q, s],
            device_id=(peer_of(orders[p][s]), my_var), device_id_type=MESH)

    own = rows_dev // n_var
    for t in range(QUARTERS + halvings):
        for q in range(QUARTERS):
            s = halvings - 1 - (t - q)
            if s < -1 or s > halvings - 1:
                continue
            for p in range(2):
                if s < halvings - 1:
                    ag_copy(p, q, s + 1).wait()
                if s >= 0:
                    ag_copy(p, q, s).start()
            if s == -1:
                rows = slice(q * part_rows, (q + 1) * part_rows)
                out_ref[rows, :] = full[rows, :].astype(out_ref.dtype)
        if t < 4:
            n = own // 4
            mine = s_ref[rows_at(my_var * own + t * n, n), :]
            basis = lax.dot_general(mine, aug[:, k_dim:], (((1,), (1,)), ((), ())), precision=highest,
                                    preferred_element_type=jnp.float32)
            scores_ref[t * n:(t + 1) * n, :] = (basis * math.sqrt(total_rows)).astype(scores_ref.dtype)


def factor_and_project(partial_sketch, col_mean, factor, records, n_rec, n_var, total_rows):
    rows_dev, k_dim = partial_sketch.shape
    columns = records.shape[1]
    groups = rec_groups(n_rec)
    orders, halvings = stage_plan(n_rec, columns)
    n_stages = len(orders[0])
    width, got_width = columns // 2, 0
    for s in range(n_stages):
        if s < halvings:
            width //= 2
        got_width += width
    piece = k_dim // n_var // groups[0][1]
    vmem = pl.BlockSpec(memory_space=pltpu.VMEM)
    dma = pltpu.SemaphoreType.DMA
    return pl.pallas_call(
        functools.partial(main_kernel, n_rec, n_var, total_rows),
        out_shape=(
            jax.ShapeDtypeStruct((rows_dev // n_var, k_dim), jnp.bfloat16),
            jax.ShapeDtypeStruct((k_dim, columns), jnp.bfloat16),
        ),
        in_specs=[vmem, vmem, vmem, pl.BlockSpec(memory_space=pl.ANY)],
        out_specs=(vmem, vmem),
        scratch_shapes=[
            pltpu.VMEM((rows_dev, k_dim), jnp.float32),
            pltpu.VMEM((rows_dev, k_dim), jnp.float32),
            pltpu.VMEM((2 * k_dim, rows_dev), jnp.bfloat16),
            pltpu.VMEM((2, rows_dev, TILE), jnp.bfloat16),
            pltpu.VMEM((rows_dev, TILE), jnp.bfloat16),
            pltpu.VMEM((k_dim, columns), jnp.float32),
            pltpu.VMEM((2, k_dim, got_width), jnp.float32),
            pltpu.VMEM((k_dim, columns), jnp.float32),
            pltpu.VMEM((2, k_dim, k_dim), jnp.float32),
            pltpu.VMEM((groups[0][1], piece, k_dim), jnp.float32),
            pltpu.VMEM((max(1, len(groups) - 1), 4, piece, k_dim), jnp.float32),
            pltpu.VMEM((k_dim, 2 * k_dim), jnp.float32),
            dma((2, QUARTERS, n_stages)), dma((2, QUARTERS, n_stages)),
            dma((2, QUARTERS, n_stages)), dma((2, QUARTERS, n_stages)),
            dma((len(groups) + 2, max(4, n_var))), dma((len(groups) + 2, max(4, n_var))),
            dma((CHUNKS,)), dma((CHUNKS,)), dma((2,)),
        ],
        compiler_params=pltpu.CompilerParams(collective_id=1, has_side_effects=True, vmem_limit_bytes=48 << 20),
    )(partial_sketch, col_mean[None, :], factor[None, :], records)


def local(records, test_matrix, col_types, col_groups, group_weight):
    n_rec, n_var = lax.axis_size("rec"), lax.axis_size("var")
    total_rows = records.shape[0] * n_rec
    columns = records.shape[1]
    values = records.astype(jnp.float32)
    sums = jnp.concatenate([jnp.sum(values, 0), jnp.sum(values * values, 0)]).reshape(-1, LANES)
    sums = sum_over_rec(sums, n_rec).reshape(2, columns)
    col_mean = sums[0] / total_rows
    onehot = (
        col_groups[:, None] == jnp.arange(group_weight.shape[0], dtype=jnp.int32)[None, :]
    ).astype(jnp.float32)
    col_weight = jnp.dot(onehot, group_weight, precision=highest)
    factor = column_factor(col_mean, sums[1] / total_rows, col_types, col_weight)
    scaled = ((values - col_mean) * factor).astype(jnp.bfloat16)
    partial_sketch = jnp.dot(scaled, test_matrix, preferred_element_type=jnp.float32)
    if n_var != 2:
        partial_sketch = lax.psum(partial_sketch, "var")
    return factor_and_project(partial_sketch, col_mean, factor, records, n_rec, n_var, total_rows)


def solution(mesh):
    in_specs = (P("rec", "var"), P("var", None), P("var"), P("var"), P())
    out_specs = (P(("rec", "var"), None), P(None, "var"))
    return jax.shard_map(local, mesh=mesh, in_specs=in_specs, out_specs=out_specs, check_vma=False)
```

```python
import functools
import math

import jax
import jax.numpy as jnp
from jax import lax
from jax.experimental import pallas as pl
from jax.experimental.pallas import tpu as pltpu
from jax.sharding import PartitionSpec as P

epsilon = 1e-05
highest = lax.Precision.HIGHEST
MESH = pl.DeviceIdType.MESH
LANES = 128
BLOCK = 64
QUARTERS = 4
TILE = 256
CHUNKS = 4


def column_factor(col_mean, col_square, col_types, col_weight):
    spread = col_square - col_mean * col_mean
    picked = jnp.where(col_types == 1, lax.rsqrt(col_mean + epsilon), lax.rsqrt(spread + epsilon))
    return picked * col_weight


def rec_groups(n_rec):
    groups, shift = [], 1
    while shift < n_rec:
        size = min(4, n_rec // shift)
        groups.append((shift, size))
        shift *= size
    return groups


def group_place(me, shift, size):
    return lax.rem(lax.div(me, shift), size)


def greet(me, groups, my_var, n_var):
    barrier = pltpu.get_barrier_semaphore()
    count = 0
    for shift, size in groups:
        place = group_place(me, shift, size)
        for k in range(1, size):
            other = me + (lax.rem(place + k, size) - place) * shift
            pl.semaphore_signal(barrier, inc=1, device_id=(other, my_var), device_id_type=MESH)
            count += 1
    for k in range(1, n_var):
        pl.semaphore_signal(barrier, inc=1, device_id=(me, lax.rem(my_var + k, n_var)), device_id_type=MESH)
        count += 1
    pl.semaphore_wait(barrier, count)


def group_start(value, buf, send_sem, recv_sem, me, my_var, shift, size):
    place = group_place(me, shift, size)
    buf[place] = value
    copies = []
    for k in range(1, size):
        other = me + (lax.rem(place + k, size) - place) * shift
        copy = pltpu.make_async_remote_copy(
            src_ref=buf.at[place], dst_ref=buf.at[place], send_sem=send_sem.at[k], recv_sem=recv_sem.at[k],
            device_id=(other, my_var), device_id_type=MESH)
        copy.start()
        copies.append(copy)
    return copies


def group_finish(buf, copies):
    for copy in copies:
        copy.wait()
    total = buf[0]
    for i in range(1, len(copies) + 1):
        total = total + buf[i]
    return total


def stats_kernel(n_rec, x_ref, o_ref, buf, send_sem, recv_sem):
    me, my_var = lax.axis_index("rec"), lax.axis_index("var")
    groups = rec_groups(n_rec)
    greet(me, groups, my_var, 1)
    current = x_ref[...]
    for g, (shift, size) in enumerate(groups):
        sent = group_start(current, buf.at[g], send_sem.at[g], recv_sem.at[g], me, my_var, shift, size)
        current = group_finish(buf.at[g], sent)
    o_ref[...] = current


def sum_over_rec(x, n_rec):
    n_groups = len(rec_groups(n_rec))
    return pl.pallas_call(
        functools.partial(stats_kernel, n_rec),
        out_shape=jax.ShapeDtypeStruct(x.shape, x.dtype),
        in_specs=[pl.BlockSpec(memory_space=pltpu.VMEM)],
        out_specs=pl.BlockSpec(memory_space=pltpu.VMEM),
        scratch_shapes=[
            pltpu.VMEM((n_groups, 4) + x.shape, jnp.float32),
            pltpu.SemaphoreType.DMA((n_groups, 4)),
            pltpu.SemaphoreType.DMA((n_groups, 4)),
        ],
        compiler_params=pltpu.CompilerParams(collective_id=0, has_side_effects=True, vmem_limit_bytes=16 << 20),
    )(x)


def rows_at(start, size):
    return pl.ds(pl.multiple_of(start, 8), size)


def lanes_at(start, size):
    return pl.ds(pl.multiple_of(start, LANES), size)


def factor_block(block, between):
    tiles_n = BLOCK // 8
    lane = lax.broadcasted_iota(jnp.int32, (8, LANES), 1)
    row = lax.broadcasted_iota(jnp.int32, (8, LANES), 0)
    tiles = []
    for t in range(tiles_n):
        eye = (lane == row + (BLOCK + 8 * t)).astype(jnp.float32)
        tiles.append(jnp.where(lane < BLOCK, block[8 * t:8 * t + 8, :], eye))
    for j in range(BLOCK - 1):
        if j in (BLOCK // 4, BLOCK // 2, 3 * BLOCK // 4):
            between()
        own, sub = j // 8, j % 8
        pivot_row = tiles[own][sub:sub + 1, :]
        scaled_row = pivot_row / pivot_row[:, j:j + 1]
        if sub < 7:
            below = jnp.where(row > sub, jnp.broadcast_to(tiles[own][:, j:j + 1], (8, LANES)), 0.0)
            tiles[own] = tiles[own] - below * scaled_row
        for t in range(own + 1, tiles_n):
            tiles[t] = tiles[t] - tiles[t][:, j:j + 1] * scaled_row
    done = []
    for t in range(tiles_n):
        pivots = jnp.sum(jnp.where(lane == row + 8 * t, tiles[t], 0.0), axis=1, keepdims=True)
        done.append(tiles[t] / jnp.sqrt(pivots))
    whole = jnp.concatenate(done, axis=0)
    return pltpu.roll(whole, BLOCK, axis=1)[:, :BLOCK]


def stage_plan(n_rec, columns):
    bits = n_rec.bit_length() - 1
    high = list(range(bits - 1, 1, -1))
    orders = [[0, 1] + high, [1, 0] + high]
    halvings = min(bits, (columns // (2 * LANES)).bit_length() - 1)
    return orders, halvings


def main_kernel(n_rec, n_var, total_rows, part_ref, mean_ref, factor_ref, rec_ref, scores_ref, out_ref,
                s_ref, s_got, s_pair, raw, tile, y_buf, got, full, gram, gram_rs, gram_ar, aug,
                rs_send, rs_recv, ag_send, ag_recv, g_send, g_recv, s_send, s_recv, raw_sem):
    me, my_var = lax.axis_index("rec"), lax.axis_index("var")
    k_dim, columns = y_buf.shape
    groups = rec_groups(n_rec)
    orders, halvings = stage_plan(n_rec, columns)
    n_stages = len(orders[0])
    part_cols = columns // 2
    part_rows = k_dim // QUARTERS
    n_tiles = columns // TILE
    rows_dev = s_ref.shape[0]
    chunk = rows_dev // CHUNKS

    def tile_at(i):
        quarter = n_tiles // 4
        turn = lax.div(jnp.int32(i), quarter)
        part, stays = lax.rem(turn, 2), lax.div(turn, 2)
        bits = [lax.rem(lax.div(me, 1 << orders[p][0]), 2) for p in range(2)]
        bit = bits[0] + part * (bits[1] - bits[0])
        which = stays * bit + (1 - stays) * (1 - bit)
        return (part * 2 + which) * quarter + lax.rem(jnp.int32(i), quarter)

    def raw_copy(i, slot):
        return pltpu.make_async_copy(rec_ref.at[:, lanes_at(tile_at(i) * TILE, TILE)], raw.at[slot], raw_sem.at[slot])

    raw_copy(0, 0).start()
    greet(me, groups, my_var, n_var)

    def sketch_copy(c):
        rows = pl.ds(c * chunk, chunk)
        return pltpu.make_async_remote_copy(
            src_ref=part_ref.at[rows, :], dst_ref=s_got.at[rows, :], send_sem=s_send.at[c], recv_sem=s_recv.at[c],
            device_id=(me, 1 - my_var), device_id_type=MESH)

    if n_var == 2:
        for c in range(CHUNKS):
            sketch_copy(c).start()

    def bit_of(j):
        return lax.rem(lax.div(me, 1 << j), 2)

    def peer_of(j):
        return me + (1 - 2 * bit_of(j)) * (1 << j)

    bases = []
    for p in range(2):
        base, held, width = [jnp.int32(p * part_cols)], [part_cols], part_cols
        for s in range(halvings):
            width //= 2
            base.append(base[-1] + bit_of(orders[p][s]) * width)
            held.append(width)
        for s in range(halvings, n_stages):
            base.append(base[-1])
            held.append(width)
        bases.append((base, held))
    got_at, at = [], 0
    for s in range(n_stages):
        got_at.append(at)
        at += bases[0][1][s + 1]

    def rs_copy(p, q, s):
        base, held = bases[p]
        width = held[s + 1]
        if s < halvings:
            start = base[s] + (1 - bit_of(orders[p][s])) * width
        else:
            start = base[s]
        rows = pl.ds(q * part_rows, part_rows)
        return pltpu.make_async_remote_copy(
            src_ref=y_buf.at[rows, lanes_at(start, width)],
            dst_ref=got.at[p, rows, pl.ds(got_at[s], width)],
            send_sem=rs_send.at[p, q, s], recv_sem=rs_recv.at[p, q, s],
            device_id=(peer_of(orders[p][s]), my_var), device_id_type=MESH)

    def rs_step(t):
        for q in range(QUARTERS):
            s = t - q
            if s < 0 or s > n_stages:
                continue
            for p in range(2):
                if s > 0:
                    rs_copy(p, q, s - 1).wait()
                    base, held = bases[p]
                    rows = pl.ds(q * part_rows, part_rows)
                    lanes = lanes_at(base[s], held[s])
                    y_buf[rows, lanes] = y_buf[rows, lanes] + got[p, rows, pl.ds(got_at[s - 1], held[s])]
                if 0 < s < n_stages:
                    rs_copy(p, q, s).start()

    def rs_begin(p, q):
        rs_copy(p, q, 0).start()

    n_steps = QUARTERS + n_stages - 1
    rs_left = list(range(1, n_steps + 1))

    n_calls = 5 * (k_dim // BLOCK) - 1
    calls = []

    def advance():
        calls.append(len(calls))
        while rs_left and (n_steps - len(rs_left)) * n_calls < len(calls) * n_steps:
            rs_step(rs_left.pop(0))

    total = jnp.zeros((k_dim, k_dim), jnp.float32)
    for c in range(CHUNKS):
        rows = pl.ds(c * chunk, chunk)
        part = part_ref[rows, :]
        if n_var == 2:
            sketch_copy(c).wait()
            part = part + s_got[rows, :]
        s_ref[rows, :] = part
        turned = part.T
        upper = turned.astype(jnp.bfloat16)
        s_pair[:k_dim, rows] = upper
        s_pair[k_dim:, rows] = (turned - upper.astype(jnp.float32)).astype(jnp.bfloat16)
        total = total + jnp.dot(turned, part, precision=highest, preferred_element_type=jnp.float32)
    gram[0] = total

    def products(first, last):
        def one(i, carry):
            slot = lax.rem(i, 2)

            @pl.when(i + 1 < n_tiles)
            def _():
                raw_copy(i + 1, 1 - slot).start()

            raw_copy(i, slot).wait()
            lanes = lanes_at(tile_at(i) * TILE, TILE)
            mean, factor = mean_ref[:, lanes], factor_ref[:, lanes]
            for c in range(CHUNKS):
                rows = pl.ds(c * chunk, chunk)
                tile[rows, :] = ((raw[slot, rows, :].astype(jnp.float32) - mean) * factor).astype(jnp.bfloat16)
            pair = jnp.dot(s_pair[...], tile[...], preferred_element_type=jnp.float32)
            y_buf[:, lanes] = pair[:k_dim] + pair[k_dim:]
            return carry

        lax.fori_loop(first, last, one, 0)

    half = k_dim // n_var
    shift, size = groups[0]
    piece = half // size
    place = group_place(me, shift, size)
    cuts = [n_tiles * i // 4 for i in range(5)]
    copies = []
    for k in range(1, size):
        other_place = lax.rem(place + k, size)
        copy = pltpu.make_async_remote_copy(
            src_ref=gram.at[0, rows_at(my_var * half + other_place * piece, piece), :],
            dst_ref=gram_rs.at[place],
            send_sem=g_send.at[0, k], recv_sem=g_recv.at[0, k],
            device_id=(me + (other_place - place) * shift, my_var), device_id_type=MESH)
        copy.start()
        copies.append(copy)
    own_rows = rows_at(my_var * half + place * piece, piece)
    gram_rs[place] = gram[0, own_rows, :]
    products(cuts[0], cuts[1])
    for copy in copies:
        copy.wait()
    current = gram_rs[0]
    for i in range(1, size):
        current = current + gram_rs[i]
    for g in range(1, len(groups)):
        sent = group_start(current, gram_ar.at[g - 1], g_send.at[g], g_recv.at[g], me, my_var, *groups[g])
        if g == 1:
            products(cuts[1], cuts[2])
        current = group_finish(gram_ar.at[g - 1], sent)
    gram[1, own_rows, :] = current
    copies = []
    last = len(groups)
    for k in range(1, size):
        other_place = lax.rem(place + k, size)
        copy = pltpu.make_async_remote_copy(
            src_ref=gram.at[1, own_rows, :], dst_ref=gram.at[1, own_rows, :],
            send_sem=g_send.at[last, k], recv_sem=g_recv.at[last, k],
            device_id=(me + (other_place - place) * shift, my_var), device_id_type=MESH)
        copy.start()
        copies.append(copy)
    for q in range(QUARTERS):
        for p in range(2):
            rs_begin(p, q)
    products(cuts[2], cuts[3])
    for copy in copies:
        copy.wait()
    copies = []
    half_rows = rows_at(my_var * half, half)
    for k in range(1, n_var):
        copy = pltpu.make_async_remote_copy(
            src_ref=gram.at[1, half_rows, :], dst_ref=gram.at[1, half_rows, :],
            send_sem=g_send.at[last + 1, k], recv_sem=g_recv.at[last + 1, k],
            device_id=(me, lax.rem(my_var + k, n_var)), device_id_type=MESH)
        copy.start()
        copies.append(copy)
    products(cuts[3], cuts[4])
    for copy in copies:
        copy.wait()

    aug[:, :k_dim] = gram[1]
    wide_row = lax.broadcasted_iota(jnp.int32, (k_dim, k_dim), 0)
    wide_lane = lax.broadcasted_iota(jnp.int32, (k_dim, k_dim), 1)
    aug[:, k_dim:] = (wide_row == wide_lane).astype(jnp.float32)
    n_blocks = k_dim // BLOCK
    for b in range(n_blocks):
        rows = slice(b * BLOCK, (b + 1) * BLOCK)
        lane_at = b * BLOCK // LANES * LANES
        block = aug[rows, lane_at:lane_at + LANES]
        if b * BLOCK != lane_at:
            block = pltpu.roll(block, LANES - BLOCK, axis=1)
        inverse = factor_block(block, advance)
        advance()
        solved = jnp.dot(inverse, aug[rows, :], precision=highest, preferred_element_type=jnp.float32)
        aug[rows, :] = solved
        if b + 1 < n_blocks:
            change = lax.dot_general(solved[:, :k_dim], solved, (((0,), (0,)), ((), ())), precision=highest,
                                     preferred_element_type=jnp.float32)
            rest = slice((b + 1) * BLOCK, k_dim)
            aug[rest, :] = aug[rest, :] - change[rest, :]
            advance()
    for t in rs_left:
        rs_step(t)

    for p in range(2):
        base, held = bases[p]
        lanes = lanes_at(base[-1], held[-1])
        full[:, lanes] = jnp.dot(aug[:, k_dim:], y_buf[:, lanes], precision=highest,
                                 preferred_element_type=jnp.float32) * (1.0 / math.sqrt(total_rows))

    def ag_copy(p, q, s):
        base, held = bases[p]
        place_now = (pl.ds(q * part_rows, part_rows), lanes_at(base[s + 1], held[s + 1]))
        return pltpu.make_async_remote_copy(
            src_ref=full.at[place_now], dst_ref=full.at[place_now],
            send_sem=ag_send.at[p, q, s], recv_sem=ag_recv.at[p, q, s],
            device_id=(peer_of(orders[p][s]), my_var), device_id_type=MESH)

    own = rows_dev // n_var
    for t in range(QUARTERS + halvings):
        for q in range(QUARTERS):
            s = halvings - 1 - (t - q)
            if s < -1 or s > halvings - 1:
                continue
            for p in range(2):
                if s < halvings - 1:
                    ag_copy(p, q, s + 1).wait()
                if s >= 0:
                    ag_copy(p, q, s).start()
            if s == -1:
                rows = slice(q * part_rows, (q + 1) * part_rows)
                out_ref[rows, :] = full[rows, :].astype(out_ref.dtype)
        if t < 4:
            n = own // 4
            mine = s_ref[rows_at(my_var * own + t * n, n), :]
            basis = lax.dot_general(mine, aug[:, k_dim:], (((1,), (1,)), ((), ())), precision=highest,
                                    preferred_element_type=jnp.float32)
            scores_ref[t * n:(t + 1) * n, :] = (basis * math.sqrt(total_rows)).astype(scores_ref.dtype)


def factor_and_project(partial_sketch, col_mean, factor, records, n_rec, n_var, total_rows):
    rows_dev, k_dim = partial_sketch.shape
    columns = records.shape[1]
    groups = rec_groups(n_rec)
    orders, halvings = stage_plan(n_rec, columns)
    n_stages = len(orders[0])
    width, got_width = columns // 2, 0
    for s in range(n_stages):
        if s < halvings:
            width //= 2
        got_width += width
    piece = k_dim // n_var // groups[0][1]
    vmem = pl.BlockSpec(memory_space=pltpu.VMEM)
    dma = pltpu.SemaphoreType.DMA
    return pl.pallas_call(
        functools.partial(main_kernel, n_rec, n_var, total_rows),
        out_shape=(
            jax.ShapeDtypeStruct((rows_dev // n_var, k_dim), jnp.bfloat16),
            jax.ShapeDtypeStruct((k_dim, columns), jnp.bfloat16),
        ),
        in_specs=[vmem, vmem, vmem, pl.BlockSpec(memory_space=pl.ANY)],
        out_specs=(vmem, vmem),
        scratch_shapes=[
            pltpu.VMEM((rows_dev, k_dim), jnp.float32),
            pltpu.VMEM((rows_dev, k_dim), jnp.float32),
            pltpu.VMEM((2 * k_dim, rows_dev), jnp.bfloat16),
            pltpu.VMEM((2, rows_dev, TILE), jnp.bfloat16),
            pltpu.VMEM((rows_dev, TILE), jnp.bfloat16),
            pltpu.VMEM((k_dim, columns), jnp.float32),
            pltpu.VMEM((2, k_dim, got_width), jnp.float32),
            pltpu.VMEM((k_dim, columns), jnp.float32),
            pltpu.VMEM((2, k_dim, k_dim), jnp.float32),
            pltpu.VMEM((groups[0][1], piece, k_dim), jnp.float32),
            pltpu.VMEM((max(1, len(groups) - 1), 4, piece, k_dim), jnp.float32),
            pltpu.VMEM((k_dim, 2 * k_dim), jnp.float32),
            dma((2, QUARTERS, n_stages)), dma((2, QUARTERS, n_stages)),
            dma((2, QUARTERS, n_stages)), dma((2, QUARTERS, n_stages)),
            dma((len(groups) + 2, max(4, n_var))), dma((len(groups) + 2, max(4, n_var))),
            dma((CHUNKS,)), dma((CHUNKS,)), dma((2,)),
        ],
        compiler_params=pltpu.CompilerParams(collective_id=1, has_side_effects=True, vmem_limit_bytes=48 << 20),
    )(partial_sketch, col_mean[None, :], factor[None, :], records)


def local(records, test_matrix, col_types, col_groups, group_weight):
    n_rec, n_var = lax.axis_size("rec"), lax.axis_size("var")
    total_rows = records.shape[0] * n_rec
    columns = records.shape[1]
    values = records.astype(jnp.float32)
    sums = jnp.concatenate([jnp.sum(values, 0), jnp.sum(values * values, 0)]).reshape(-1, LANES)
    sums = sum_over_rec(sums, n_rec).reshape(2, columns)
    col_mean = sums[0] / total_rows
    onehot = (
        col_groups[:, None] == jnp.arange(group_weight.shape[0], dtype=jnp.int32)[None, :]
    ).astype(jnp.float32)
    col_weight = jnp.dot(onehot, group_weight, precision=highest)
    factor = column_factor(col_mean, sums[1] / total_rows, col_types, col_weight)
    scaled = ((values - col_mean) * factor).astype(jnp.bfloat16)
    partial_sketch = jnp.dot(scaled, test_matrix, preferred_element_type=jnp.float32)
    if n_var != 2:
        partial_sketch = lax.psum(partial_sketch, "var")
    return factor_and_project(partial_sketch, col_mean, factor, records, n_rec, n_var, total_rows)


def solution(mesh):
    in_specs = (P("rec", "var"), P("var", None), P("var"), P("var"), P())
    out_specs = (P(("rec", "var"), None), P(None, "var"))
    return jax.shard_map(local, mesh=mesh, in_specs=in_specs, out_specs=out_specs, check_vma=False)
```
